32 devices in a mesh: leaf: 16 (over z, y, x), grp: 2 (over core).
Axes of the slice: x: 2, y: 2, z: 4, core: 2. Of those that a mesh axis runs over, the one named last changes fastest.
Arguments:
- diag_block: float32 [6144, 384], P(('leaf', 'grp')), as said below
- generator: float32 [6144, 128], P(('leaf', 'grp')), may hold values from -0.3125 to 0.3125
- right_sides: float32 [6144, 256], P('leaf', 'grp'), may hold values from -6 to 6
- interp_first: float32 [3072, 384], P('leaf'), may hold values from -0.109375 to 0.109375
- interp_second: float32 [1536, 384], P('leaf'), may hold values from -0.109375 to 0.109375
- interp_third: float32 [768, 384], P('leaf'), may hold values from -0.109375 to 0.109375
- interp_fourth: float32 [384, 384], P('leaf'), may hold values from -0.109375 to 0.109375
- node_ranks: int32 [16], replicated, may hold values from 128 to 384, as said below
Outputs:
- reduced_block: float32 [6144, 384], P(('leaf', 'grp'))
- reduced_generator: float32 [6144, 128], P(('leaf', 'grp'))
- reduced_rhs: float32 [6144, 256], P('leaf', 'grp')
The draws below stay inside these ranges and needn't reach their ends.
Inputs may be any that keep to these rules, and one draw needn't show every extreme that they name: Every 384 x 384 block of diag_block is symmetric positive definite with smallest eigenvalue at least 0.002. `node_ranks`: some base node has rank 384 and some has rank 128.
All inputs are finite; a program needn't handle non-finite values.
Results may differ from the reference program's by a relative error of at most 0.0005.
Values sent between devices are 32-bit elements; how exact they have to be, the bound alone decides.
A program may use at most 64 MiB of HBM per device.

```python
import jax
import jax.numpy as jnp
from jax import lax

R = 384
K = 128
LEVELS = 4
RMIN = 128
BASE_NODES = 16
NRHS = 256


def draw_diag_block(key, part):
    strong_key = jax.random.fold_in(key, 11)
    weak_key = jax.random.fold_in(key, 12)
    column_count = R // 8
    strong_factor = jax.random.randint(strong_key, (BASE_NODES, R, column_count), -7, 8).astype(jnp.float32)
    weak_factor = jax.random.randint(weak_key, (BASE_NODES, R, R), -7, 8).astype(jnp.float32)
    strong_gram = jnp.einsum('nij,nkj->nik', strong_factor, strong_factor, precision=lax.Precision.HIGHEST)
    weak_gram = jnp.einsum('nij,nkj->nik', weak_factor, weak_factor, precision=lax.Precision.HIGHEST)
    variance = 56.0 / 3.0
    lowest_level = 0.002
    strong_weight = 4.0
    identity = jnp.eye(R, dtype=jnp.float32)
    blocks = lowest_level * identity[None] + weak_gram * (lowest_level / (R * variance)) + strong_gram * (strong_weight / (R * variance))
    return blocks.reshape(BASE_NODES * R, R).astype(jnp.float32)


def draw_node_ranks(key, part):
    values = jax.random.randint(jax.random.fold_in(key, 21), (BASE_NODES,), RMIN, R + 1)
    values = values.at[0].set(R).at[1].set(RMIN)
    return values.astype(jnp.int32)


def level_of(rng, shape, cuts, low, high):
    def one(position, parts):
        steps = jax.random.uniform(jax.random.fold_in(jax.random.fold_in(rng, 6), position), (parts,), jnp.float32, low / len(cuts), high / len(cuts))
        return jnp.repeat(jnp.exp(steps), shape[position] // parts).reshape((-1,) + (1,) * (len(shape) - position - 1))

    level = one(*cuts[0])
    for cut in cuts[1:]:
        level = level * one(*cut)
    return level


def gaussian(rng, shape, width, bound, split=(), kind=jnp.bfloat16):
    gain = level_of(rng, shape, split, -0.22, 0.18) if split else 1.0
    drawn = jax.random.normal(rng, shape, jnp.float32) * width * gain
    return jnp.minimum(jnp.maximum(drawn, -bound), bound).astype(kind)


def setup_inputs(seed: int = 0) -> dict:
    keys = jax.random.split(jax.random.key(seed), 9)
    return {
        "diag_block": draw_diag_block(jax.random.fold_in(keys[8], 71), 0),
        "generator": gaussian(keys[1], (BASE_NODES * R, K), R ** -0.5, 0.3125, ((0, 32),), jnp.float32),
        "right_sides": gaussian(keys[2], (BASE_NODES * R, NRHS), 1.0, 6.0, ((0, 16), (1, 2)), jnp.float32),
        "interp_first": gaussian(keys[3], (BASE_NODES * R // 2, R), (8 * R) ** -0.5, 0.109375, ((0, 16),), jnp.float32),
        "interp_second": gaussian(keys[4], (BASE_NODES * R // 4, R), (8 * R) ** -0.5, 0.109375, ((0, 16),), jnp.float32),
        "interp_third": gaussian(keys[5], (BASE_NODES * R // 8, R), (8 * R) ** -0.5, 0.109375, ((0, 16),), jnp.float32),
        "interp_fourth": gaussian(keys[6], (BASE_NODES * R // 16, R), (8 * R) ** -0.5, 0.109375, ((0, 16),), jnp.float32),
        "node_ranks": draw_node_ranks(jax.random.fold_in(keys[8], 71), 0),
    }


def product(first_factor, second_factor):
    return jnp.dot(first_factor.astype(jnp.float32), second_factor.astype(jnp.float32), precision=lax.Precision.HIGHEST, preferred_element_type=jnp.float32)

def triangle_solve(factor, values):
    return jax.scipy.linalg.solve_triangular(factor, values, lower=True)

def mask_block(diagonal, generator_block, right_block, node_rank):
    row_ids = jnp.arange(diagonal.shape[0])[:, None]
    col_ids = jnp.arange(diagonal.shape[1])[None, :]
    inside_rows = row_ids < node_rank
    identity = jnp.where(row_ids == col_ids, 1.0, 0.0).astype(jnp.float32)
    diagonal = jnp.where(inside_rows & (col_ids < node_rank), diagonal, identity)
    generator_block = jnp.where(inside_rows, generator_block, 0.0)
    right_block = jnp.where(inside_rows, right_block, 0.0)
    return (diagonal, generator_block, right_block)

def merge_pair(low_diag, high_diag, low_gen, high_gen, low_rhs, high_rhs, mixing, low_rank, high_rank):
    row_ids = jnp.arange(mixing.shape[0])[:, None]
    col_ids = jnp.arange(mixing.shape[1])[None, :]
    mixing = jnp.where((row_ids < high_rank) & (col_ids < low_rank), mixing, 0.0)
    low_full = low_diag + product(low_gen, low_gen.T)
    high_full = high_diag + product(high_gen, high_gen.T)
    coupling = product(low_gen, high_gen.T)
    high_mixed = product(high_full, mixing)
    cross = coupling + high_mixed.T
    coupled_mixed = product(low_gen, product(high_gen.T, mixing))
    pivot = low_full + coupled_mixed + coupled_mixed.T + product(mixing.T, high_mixed)
    factor = jnp.linalg.cholesky(pivot)
    solved = triangle_solve(factor, cross)
    reduced = high_full - product(solved.T, solved)
    gen_input = low_gen + product(mixing.T, high_gen)
    new_gen = high_gen - product(solved.T, triangle_solve(factor, gen_input))
    rhs_input = low_rhs + product(mixing.T, high_rhs)
    new_rhs = high_rhs - product(solved.T, triangle_solve(factor, rhs_input))
    return (reduced, new_gen, new_rhs)

def reference(diag_block, generator, right_sides, interp_first, interp_second, interp_third, interp_fourth, node_ranks):
    node_count = diag_block.shape[0] // R
    diagonals = diag_block.reshape(node_count, R, R)
    generators = generator.reshape(node_count, R, K)
    rhs_blocks = right_sides.reshape(node_count, R, -1)
    diagonals, generators, rhs_blocks = jax.vmap(mask_block)(diagonals, generators, rhs_blocks, node_ranks)
    mixings = (interp_first, interp_second, interp_third, interp_fourth)
    for height in range(LEVELS):
        span_size = 2 ** height
        level_ranks = node_ranks.reshape(-1, span_size)[:, -1]
        mixing_blocks = mixings[height].reshape(-1, R, R)
        diagonals, generators, rhs_blocks = jax.vmap(merge_pair)(diagonals[0::2], diagonals[1::2], generators[0::2], generators[1::2], rhs_blocks[0::2], rhs_blocks[1::2], mixing_blocks, level_ranks[0::2], level_ranks[1::2])
    spread = 2 ** LEVELS
    out_block = jnp.repeat(diagonals, spread, axis=0).reshape(-1, R)
    out_gen = jnp.repeat(generators, spread, axis=0).reshape(-1, K)
    out_rhs = jnp.repeat(rhs_blocks, spread, axis=0).reshape(node_count * R, -1)
    return (out_block, out_gen, out_rhs)
```

```python
import functools

import jax
import jax.numpy as jnp
from jax import lax
from jax.experimental import pallas as pl
from jax.experimental.pallas import tpu as pltpu
from jax.sharding import PartitionSpec as P

LEVELS = 4
LANES = 128
PANEL = 32
HIGHEST = lax.Precision.HIGHEST


def swapped(block, axis, bit):
    count = lax.axis_size(axis)
    route = []
    for low in range(count):
        high = low | 1 << bit
        if high != low and high < count:
            route += [(low, high), (high, low)]
    return lax.ppermute(block, axis, route)


def dot_nn(a, b):
    return lax.dot_general(a, b, (((1,), (0,)), ((), ())), precision=HIGHEST, preferred_element_type=jnp.float32)


def dot_tn(a, b):
    return lax.dot_general(a, b, (((0,), (0,)), ((), ())), precision=HIGHEST, preferred_element_type=jnp.float32)


def dot_nt(a, b):
    return lax.dot_general(a, b, (((1,), (1,)), ((), ())), precision=HIGHEST, preferred_element_type=jnp.float32)


def inverse_factor(slab):
    groups = PANEL // 8
    lane = lax.broadcasted_iota(jnp.int32, (8, LANES), 1)
    row = lax.broadcasted_iota(jnp.int32, (8, LANES), 0)
    state = []
    for g in range(groups):
        unit = jnp.where(lane == row + (PANEL + 8 * g), 1.0, 0.0)
        state.append(jnp.where(lane < PANEL, slab[8 * g : 8 * g + 8], unit))
    for q in range(groups):
        cols = {}
        for j in range(8):
            for g in range(q, groups):
                at = 8 * q + j
                cols[g, j] = jnp.broadcast_to(state[g][:, at : at + 1], (8, LANES))
        pivots = cols[q, 0]
        for j in range(8):
            if j:
                pivots = jnp.where(row == j, cols[q, j], pivots)
            inv = 1.0 / jnp.broadcast_to(cols[q, j][j : j + 1], (8, LANES))
            line = jnp.broadcast_to(state[q][j : j + 1], (8, LANES)) * inv
            factors = [jnp.broadcast_to(cols[q, k][j : j + 1], (8, LANES)) * inv for k in range(j + 1, 8)]
            for g in range(q, groups):
                if g == q and j == 7:
                    continue
                mult = cols[g, j]
                if g == q:
                    mult = jnp.where(row > j, mult, 0.0)
                for k in range(j + 1, 8):
                    cols[g, k] = cols[g, k] - mult * factors[k - j - 1]
                state[g] = state[g] - mult * line
        state[q] = state[q] * lax.rsqrt(pivots)
    whole = jnp.concatenate(state, axis=0)
    return whole[:, PANEL : 2 * PANEL]


def merge_kernel(info, own_b, own_g, own_y, peer_b, peer_g, peer_y, mix, out_b, out_g, out_y, work, high):
    size = own_b.shape[0]
    wide = size + own_g.shape[1] + own_y.shape[1]
    gen_w = own_g.shape[1]
    upper = info[0] == 1
    low_rank = info[1]
    high_rank = info[2]
    row_ids = lax.broadcasted_iota(jnp.int32, (size, size), 0)
    col_ids = lax.broadcasted_iota(jnp.int32, (size, size), 1)
    mixing = jnp.where((row_ids < high_rank) & (col_ids < low_rank), mix[...], 0.0)
    high[:, :size] = jnp.where(upper, own_b[...], peer_b[...])
    high[:, size : size + gen_w] = jnp.where(upper, own_g[...], peer_g[...])
    high[:, size + gen_w :] = jnp.where(upper, own_y[...], peer_y[...])
    low_b = jnp.where(upper, peer_b[...], own_b[...])
    low_g = jnp.where(upper, peer_g[...], own_g[...])
    low_y = jnp.where(upper, peer_y[...], own_y[...])
    mixed = dot_tn(mixing, high[...])
    high_gen = high[:, size : size + gen_w]
    w_gen = low_g + mixed[:, size : size + gen_w]
    work[:, size + size : size + size + gen_w] = w_gen
    work[:, size + size + gen_w :] = low_y + mixed[:, size + gen_w :]
    work[:, size : 2 * size] = mixed[:, :size] + dot_nt(w_gen, high_gen)
    work[:, :size] = low_b + dot_nn(mixed[:, :size], mixing) + dot_nt(w_gen, w_gen)
    high[:, :size] = high[:, :size] + dot_nt(high_gen, high_gen)

    for chunk in range(size // LANES):
        base = chunk * LANES
        steps = jnp.clip((low_rank - base + PANEL - 1) // PANEL, 0, LANES // PANEL)

        def panel(q, carry, base=base):
            start = pl.multiple_of(base + q * PANEL, PANEL)
            slab = work[pl.ds(start, PANEL), base : base + LANES]
            slab = pltpu.roll(slab, (LANES - q * PANEL) % LANES, 1)
            inv = inverse_factor(slab)
            rows = dot_nn(inv, work[pl.ds(start, PANEL), base:])
            work[pl.ds(start, PANEL), base:] = rows
            ids = lax.broadcasted_iota(jnp.int32, (PANEL, LANES), 1)
            left = jnp.where(ids >= (q + 1) * PANEL, rows[:, :LANES], 0.0)
            work[base : base + LANES, base:] = work[base : base + LANES, base:] - dot_tn(left, rows)
            return carry

        lax.fori_loop(0, steps, panel, 0)
        after = base + LANES
        if after < size:

            @pl.when(low_rank > after)
            def _(base=base, after=after):
                done = work[base:after, after:]
                work[after:size, after:] = work[after:size, after:] - dot_tn(done[:, : size - after], done)

    solved = work[:, size:]
    result = high[...] - dot_tn(solved[:, :size], solved)
    out_b[...] = result[:, :size]
    out_g[...] = result[:, size : size + gen_w]
    out_y[...] = result[:, size + gen_w :]


def merge(info, own, peer, mixing):
    size, gen_w, rhs_w = own[0].shape[0], own[1].shape[1], own[2].shape[1]
    wide = size + gen_w + rhs_w
    vmem = pl.BlockSpec(memory_space=pltpu.VMEM)
    return pl.pallas_call(
        merge_kernel,
        out_shape=[jax.ShapeDtypeStruct(x.shape, jnp.float32) for x in own],
        in_specs=[pl.BlockSpec(memory_space=pltpu.SMEM)] + [vmem] * 7,
        out_specs=[vmem] * 3,
        scratch_shapes=[
            pltpu.VMEM((size, size + wide), jnp.float32),
            pltpu.VMEM((size, wide), jnp.float32),
        ],
        compiler_params=pltpu.CompilerParams(vmem_limit_bytes=40 * 2**20),
        cost_estimate=pl.CostEstimate(flops=6 * 10**9, bytes_accessed=4 * 2**20, transcendentals=0),
    )(info, *own, *peer, mixing)


def rank_at(node_ranks, index_value):
    entries = jnp.arange(node_ranks.shape[0])
    return jnp.sum(jnp.where(entries == index_value, node_ranks, 0))


def child_ranks(node_ranks, position, height):
    first_base = position >> height + 1 << height + 1
    low_rank = rank_at(node_ranks, first_base + 2**height - 1)
    high_rank = rank_at(node_ranks, first_base + 2 ** (height + 1) - 1)
    return (low_rank, high_rank)


def mask_rows(diagonal, generator_block, right_block, node_rank):
    row_ids = jnp.arange(diagonal.shape[0])[:, None]
    col_ids = jnp.arange(diagonal.shape[1])[None, :]
    inside_rows = row_ids < node_rank
    identity = jnp.where(row_ids == col_ids, 1.0, 0.0).astype(jnp.float32)
    diagonal = jnp.where(inside_rows & (col_ids < node_rank), diagonal, identity)
    generator_block = jnp.where(inside_rows, generator_block, 0.0)
    return (diagonal, generator_block, jnp.where(inside_rows, right_block, 0.0))


def on_device(diag_block, generator, right_sides, interp_first, interp_second, interp_third, interp_fourth, node_ranks):
    position = lax.axis_index("leaf")
    member = lax.axis_index("grp")
    share = diag_block.shape[0]
    leaves = lax.axis_size("leaf")
    base_rank = rank_at(node_ranks, position)
    pieces = [interp_first, interp_second, interp_third, interp_fourth]
    diag_full = lax.all_gather(diag_block, "grp", axis=0, tiled=True)
    gen_full = lax.all_gather(generator, "grp", axis=0, tiled=True)
    blocks = []
    for height in range(LEVELS):
        span = 2 ** (height + 1)
        groups = [list(range(first, first + span)) for first in range(0, leaves, span)]
        blocks.append(lax.all_gather(pieces[height], "leaf", axis=0, tiled=True, axis_index_groups=groups))
    now = mask_rows(diag_full, gen_full, right_sides, base_rank)
    for height in range(LEVELS):
        peer = swapped(now, "leaf", height)
        is_upper = position >> height & 1
        low_rank, high_rank = child_ranks(node_ranks, position, height)
        info = jnp.stack([is_upper, low_rank, high_rank]).astype(jnp.int32)
        now = merge(info, now, peer, blocks[height])
    out_block = lax.dynamic_slice_in_dim(now[0], member * share, share, 0)
    out_gen = lax.dynamic_slice_in_dim(now[1], member * share, share, 0)
    return (out_block, out_gen, now[2])


def solution(mesh):
    placed = (
        P(("leaf", "grp"), None),
        P(("leaf", "grp"), None),
        P("leaf", "grp"),
        P("leaf", None),
        P("leaf", None),
        P("leaf", None),
        P("leaf", None),
        P(),
    )
    return jax.shard_map(
        on_device,
        mesh=mesh,
        in_specs=placed,
        out_specs=(P(("leaf", "grp"), None), P(("leaf", "grp"), None), P("leaf", "grp")),
        check_vma=False,
    )
```

```python
import functools

import jax
import jax.numpy as jnp
from jax import lax
from jax.experimental import pallas as pl
from jax.experimental.pallas import tpu as pltpu
from jax.sharding import PartitionSpec as P

LEVELS = 4
LANES = 128
PANEL = 32
HIGHEST = lax.Precision.HIGHEST


def dot_nn(a, b):
    return lax.dot_general(a, b, (((1,), (0,)), ((), ())), precision=HIGHEST, preferred_element_type=jnp.float32)


def dot_tn(a, b):
    return lax.dot_general(a, b, (((0,), (0,)), ((), ())), precision=HIGHEST, preferred_element_type=jnp.float32)


def dot_nt(a, b):
    return lax.dot_general(a, b, (((1,), (1,)), ((), ())), precision=HIGHEST, preferred_element_type=jnp.float32)


def inverse_factor(slab):
    groups = PANEL // 8
    lane = lax.broadcasted_iota(jnp.int32, (8, LANES), 1)
    row = lax.broadcasted_iota(jnp.int32, (8, LANES), 0)
    state = []
    for g in range(groups):
        unit = jnp.where(lane == row + (PANEL + 8 * g), 1.0, 0.0)
        state.append(jnp.where(lane < PANEL, slab[8 * g : 8 * g + 8], unit))
    for q in range(groups):
        cols = {}
        for j in range(8):
            for g in range(q, groups):
                at = 8 * q + j
                cols[g, j] = jnp.broadcast_to(state[g][:, at : at + 1], (8, LANES))
        pivots = cols[q, 0]
        for j in range(8):
            if j:
                pivots = jnp.where(row == j, cols[q, j], pivots)
            inv = 1.0 / jnp.broadcast_to(cols[q, j][j : j + 1], (8, LANES))
            line = jnp.broadcast_to(state[q][j : j + 1], (8, LANES)) * inv
            factors = [jnp.broadcast_to(cols[q, k][j : j + 1], (8, LANES)) * inv for k in range(j + 1, 8)]
            for g in range(q, groups):
                if g == q and j == 7:
                    continue
                mult = cols[g, j]
                if g == q:
                    mult = jnp.where(row > j, mult, 0.0)
                for k in range(j + 1, 8):
                    cols[g, k] = cols[g, k] - mult * factors[k - j - 1]
                state[g] = state[g] - mult * line
        state[q] = state[q] * lax.rsqrt(pivots)
    whole = jnp.concatenate(state, axis=0)
    return whole[:, PANEL : 2 * PANEL]


def merge_kernel(first, slots, info, own_b, own_g, own_y, peer_b, peer_g, peer_y, mix_a, mix_b, out_b, out_g, out_y, work, high, full, mix):
    size = own_b.shape[0]
    gen_w = own_g.shape[1]
    upper = info[0] == 1
    low_rank = info[1]
    high_rank = info[2]
    part = size // len(slots)
    for which, offset, flip in slots:
        index = jnp.bitwise_xor(info[3], flip) % len(slots)
        mix[pl.ds(pl.multiple_of(index * part, part), part), :] = (mix_b if which else mix_a)[offset : offset + part, :]
    row_ids = lax.broadcasted_iota(jnp.int32, (size, size), 0)
    col_ids = lax.broadcasted_iota(jnp.int32, (size, size), 1)
    mixing = jnp.where((row_ids < high_rank) & (col_ids < low_rank), mix[...], 0.0)
    if first:
        full[...] = peer_b[...]
    else:
        for i in range(size // LANES):
            for j in range(i + 1):
                here, there = slice(i * LANES, (i + 1) * LANES), slice(j * LANES, (j + 1) * LANES)
                full[here, there] = peer_b[here, there]
                if j < i:
                    full[there, here] = peer_b[here, there].T
    high_b = jnp.where(upper, own_b[...], full[...])
    high_g = jnp.where(upper, own_g[...], peer_g[...])
    high_y = jnp.where(upper, own_y[...], peer_y[...])
    low_b = jnp.where(upper, full[...], own_b[...])
    low_g = jnp.where(upper, peer_g[...], own_g[...])
    low_y = jnp.where(upper, peer_y[...], own_y[...])
    if first:
        unit = jnp.where(row_ids == col_ids, 1.0, 0.0)
        high_b = jnp.where((row_ids < high_rank) & (col_ids < high_rank), high_b, unit)
        low_b = jnp.where((row_ids < low_rank) & (col_ids < low_rank), low_b, unit)
        gen_rows = lax.broadcasted_iota(jnp.int32, high_g.shape, 0)
        rhs_rows = lax.broadcasted_iota(jnp.int32, high_y.shape, 0)
        high_g = jnp.where(gen_rows < high_rank, high_g, 0.0)
        low_g = jnp.where(gen_rows < low_rank, low_g, 0.0)
        high_y = jnp.where(rhs_rows < high_rank, high_y, 0.0)
        low_y = jnp.where(rhs_rows < low_rank, low_y, 0.0)
    high[:, :size] = high_b
    high[:, size : size + gen_w] = high_g
    high[:, size + gen_w :] = high_y
    mixed = dot_tn(mixing, high[...])
    high_gen = high[:, size : size + gen_w]
    w_gen = low_g + mixed[:, size : size + gen_w]
    work[:, size + size : size + size + gen_w] = w_gen
    work[:, size + size + gen_w :] = low_y + mixed[:, size + gen_w :]
    work[:, size : 2 * size] = mixed[:, :size] + dot_nt(w_gen, high_gen)
    work[:, :size] = low_b + dot_nn(mixed[:, :size], mixing) + dot_nt(w_gen, w_gen)
    high[:, :size] = high[:, :size] + dot_nt(high_gen, high_gen)

    for chunk in range(size // LANES):
        base = chunk * LANES
        steps = jnp.clip((low_rank - base + PANEL - 1) // PANEL, 0, LANES // PANEL)

        def panel(q, carry, base=base):
            start = pl.multiple_of(base + q * PANEL, PANEL)
            slab = work[pl.ds(start, PANEL), base : base + LANES]
            slab = pltpu.roll(slab, (LANES - q * PANEL) % LANES, 1)
            inv = inverse_factor(slab)
            rows = dot_nn(inv, work[pl.ds(start, PANEL), base:])
            work[pl.ds(start, PANEL), base:] = rows
            ids = lax.broadcasted_iota(jnp.int32, (PANEL, LANES), 1)
            left = jnp.where(ids >= (q + 1) * PANEL, rows[:, :LANES], 0.0)
            work[base : base + LANES, base:] = work[base : base + LANES, base:] - dot_tn(left, rows)
            return carry

        lax.fori_loop(0, steps, panel, 0)
        after = base + LANES
        if after < size:

            @pl.when(low_rank > after)
            def _(base=base, after=after):
                done = work[base:after, after:]
                work[after:size, after:] = work[after:size, after:] - dot_tn(done[:, : size - after], done)

    solved = work[:, size:]
    result = high[...] - dot_tn(solved[:, :size], solved)
    out_b[...] = result[:, :size]
    out_g[...] = result[:, size : size + gen_w]
    out_y[...] = result[:, size + gen_w :]


def merge(first, slots, info, own, peer, mix_a, mix_b):
    size, gen_w, rhs_w = own[0].shape[0], own[1].shape[1], own[2].shape[1]
    wide = size + gen_w + rhs_w
    vmem = pl.BlockSpec(memory_space=pltpu.VMEM)
    return pl.pallas_call(
        functools.partial(merge_kernel, first, slots),
        out_shape=[jax.ShapeDtypeStruct(x.shape, jnp.float32) for x in own],
        in_specs=[pl.BlockSpec(memory_space=pltpu.SMEM)] + [vmem] * 8,
        out_specs=[vmem] * 3,
        scratch_shapes=[
            pltpu.VMEM((size, size + wide), jnp.float32),
            pltpu.VMEM((size, wide), jnp.float32),
            pltpu.VMEM((size, size), jnp.float32),
            pltpu.VMEM((size, size), jnp.float32),
        ],
        compiler_params=pltpu.CompilerParams(vmem_limit_bytes=40 * 2**20),
        cost_estimate=pl.CostEstimate(flops=6 * 10**9, bytes_accessed=4 * 2**20, transcendentals=0),
    )(info, *own, *peer, mix_a, mix_b)


def flipped(index, step):
    return index + step - 2 * step * ((index // step) % 2)


def greet(devices):
    barrier = pltpu.get_barrier_semaphore()
    for device in devices:
        pl.semaphore_signal(barrier, inc=1, device_id=device, device_id_type=pl.DeviceIdType.MESH)
    pl.semaphore_wait(barrier, len(devices))


class Sender:
    def __init__(self, send, recv):
        self.send, self.recv, self.used = send, recv, 0

    def __call__(self, src, dst, device):
        copy = pltpu.make_async_remote_copy(
            src_ref=src,
            dst_ref=dst,
            send_sem=self.send.at[self.used],
            recv_sem=self.recv.at[self.used],
            device_id=device,
            device_id_type=pl.DeviceIdType.MESH,
        )
        self.used += 1
        copy.start()
        return copy


def first_kernel(diag, gen, rhs, near, later, own_b, own_g, peer_b, peer_g, peer_y, peer_near, peer_later, send, recv, local):
    leaf, core = lax.axis_index("leaf"), lax.axis_index("grp")
    across, over, beside = (flipped(leaf, 1), core), (flipped(leaf, 2), core), (leaf, flipped(core, 1))
    greet([across, over, beside])
    size = own_b.shape[0]
    half = size // 2
    side = core % 2
    mine = pl.ds(pl.multiple_of(side * half, half), half)
    quarter = near.shape[0] // 2
    near_mine = pl.ds(pl.multiple_of(side * quarter, quarter), quarter)
    keep_b = pltpu.make_async_copy(diag, own_b.at[mine], local.at[0])
    keep_g = pltpu.make_async_copy(gen, own_g.at[mine], local.at[1])
    remote = Sender(send, recv)
    far = [
        (remote(diag, peer_b.at[mine], across), peer_b.at[mine]),
        (remote(near.at[near_mine], peer_near.at[near_mine], across), peer_near.at[near_mine]),
        (remote(gen, peer_g.at[mine], across), peer_g.at[mine]),
    ]
    rest = [
        remote(rhs, peer_y, across),
        remote(later, peer_later, over),
        remote(diag, own_b.at[mine], beside),
        remote(gen, own_g.at[mine], beside),
    ]
    keep_b.start()
    keep_g.start()
    for copy, place in far:
        copy.wait_recv()
        rest.append(remote(place, place, beside))
    for copy, place in far:
        copy.wait_send()
    for copy in rest:
        copy.wait()
    keep_b.wait()
    keep_g.wait()


def first_exchange(diag, gen, rhs, near, later):
    size = diag.shape[1]
    anywhere = pl.BlockSpec(memory_space=pl.ANY)
    shapes = [(size, size), (size, gen.shape[1]), (size, size), (size, gen.shape[1]), rhs.shape, near.shape, later.shape]
    return pl.pallas_call(
        first_kernel,
        out_shape=[jax.ShapeDtypeStruct(x, jnp.float32) for x in shapes],
        in_specs=[anywhere] * 5,
        out_specs=[anywhere] * 7,
        scratch_shapes=[pltpu.SemaphoreType.DMA((10,)), pltpu.SemaphoreType.DMA((10,)), pltpu.SemaphoreType.DMA((2,))],
        compiler_params=pltpu.CompilerParams(collective_id=0, has_side_effects=True),
    )(diag, gen, rhs, near, later)


def pair_kernel(step, b, g, y, peer_b, peer_g, peer_y, send, recv):
    leaf, core = lax.axis_index("leaf"), lax.axis_index("grp")
    across, beside = (flipped(leaf, step), core), (leaf, flipped(core, 1))
    greet([across, beside])
    side = core % 2
    half = g.shape[0] // 2
    mine = pl.ds(pl.multiple_of(side * half, half), half)
    remote = Sender(send, recv)
    far = []
    for t in range(3):
        row = 2 * side + (1 - side) * (0, 1, 1)[t]
        col = t * side + (1 - side) * (0, 0, 1)[t]
        rows = pl.ds(pl.multiple_of(row * LANES, LANES), LANES)
        cols = pl.ds(pl.multiple_of(col * LANES, LANES), LANES)
        far.append((remote(b.at[rows, cols], peer_b.at[rows, cols], across), peer_b.at[rows, cols]))
    far.append((remote(g.at[mine], peer_g.at[mine], across), peer_g.at[mine]))
    rest = [remote(y, peer_y, across)]
    for copy, place in far:
        copy.wait_recv()
        rest.append(remote(place, place, beside))
    for copy, place in far:
        copy.wait_send()
    for copy in rest:
        copy.wait()


def pair_exchange(height, own):
    anywhere = pl.BlockSpec(memory_space=pl.ANY)
    return pl.pallas_call(
        functools.partial(pair_kernel, 2**height),
        out_shape=[jax.ShapeDtypeStruct(x.shape, jnp.float32) for x in own],
        in_specs=[anywhere] * 3,
        out_specs=[anywhere] * 3,
        scratch_shapes=[pltpu.SemaphoreType.DMA((9,)), pltpu.SemaphoreType.DMA((9,))],
        compiler_params=pltpu.CompilerParams(collective_id=height, has_side_effects=True),
    )(*own)


def swapped(block, axis, bit):
    count = lax.axis_size(axis)
    return lax.ppermute(block, axis, [(low, low ^ 1 << bit) for low in range(count)])


def rank_at(node_ranks, index_value):
    entries = jnp.arange(node_ranks.shape[0])
    return jnp.sum(jnp.where(entries == index_value, node_ranks, 0))


def child_ranks(node_ranks, position, height):
    first_base = position >> height + 1 << height + 1
    low_rank = rank_at(node_ranks, first_base + 2**height - 1)
    high_rank = rank_at(node_ranks, first_base + 2 ** (height + 1) - 1)
    return (low_rank, high_rank)


def on_device(diag_block, generator, right_sides, interp_first, interp_second, interp_third, interp_fourth, node_ranks):
    position = lax.axis_index("leaf")
    member = lax.axis_index("grp")
    share = diag_block.shape[0]
    size = diag_block.shape[1]
    near = interp_first
    later = jnp.concatenate([interp_second, interp_third, interp_fourth], axis=0)
    rows = [x.shape[0] for x in (interp_first, interp_second, interp_third, interp_fourth)]
    infos = []
    for height in range(LEVELS):
        low_rank, high_rank = child_ranks(node_ranks, position, height)
        infos.append(jnp.stack([position >> height & 1, low_rank, high_rank, position]).astype(jnp.int32))
    diag_half, gen_half = diag_block, generator
    if 2 * share != size:
        side = member % 2
        diag_full = lax.all_gather(diag_block, "grp", axis=0, tiled=True)
        gen_full = lax.all_gather(generator, "grp", axis=0, tiled=True)
        diag_half = lax.dynamic_slice_in_dim(diag_full, side * (size // 2), size // 2, 0)
        gen_half = lax.dynamic_slice_in_dim(gen_full, side * (size // 2), size // 2, 0)
    own_b, own_g, peer_b, peer_g, peer_y, peer_near, peer_later = first_exchange(
        diag_half, gen_half, right_sides, near, later
    )
    now = (own_b, own_g, right_sides)
    peer = (peer_b, peer_g, peer_y)
    held, got = near, peer_near
    flips = [0]
    held_next = jnp.concatenate([later, peer_later], axis=0)
    got_next = swapped(held_next, "leaf", 0)
    flips_next = [0, 2]
    for height in range(LEVELS):
        bit = (0, 0, 2, 3)[height]
        width = sum(rows[height:]) if height else rows[0]
        slots = []
        for which in range(2):
            slots += [(which, i * width, flip ^ (which << bit)) for i, flip in enumerate(flips)]
        now = merge(height == 0, slots, infos[height], now, peer, held, got)
        if height + 1 < LEVELS:
            held, got, flips = held_next, got_next, flips_next
            peer = pair_exchange(height + 1, now)
            if height + 2 < LEVELS:
                skip, wide = rows[height + 1], sum(rows[height + 1 :])
                pieces = []
                for array in (held, got):
                    pieces += [array[i * wide + skip : (i + 1) * wide] for i in range(len(flips))]
                held_next = jnp.concatenate(pieces, axis=0)
                got_next = swapped(held_next, "leaf", height + 2)
                flips_next = flips + [flip ^ (1 << (0, 0, 2, 3)[height + 1]) for flip in flips]
    out_block = lax.dynamic_slice_in_dim(now[0], member % (size // share) * share, share, 0)
    out_gen = lax.dynamic_slice_in_dim(now[1], member % (size // share) * share, share, 0)
    return (out_block, out_gen, now[2])


def solution(mesh):
    placed = (
        P(("leaf", "grp"), None),
        P(("leaf", "grp"), None),
        P("leaf", "grp"),
        P("leaf", None),
        P("leaf", None),
        P("leaf", None),
        P("leaf", None),
        P(),
    )
    return jax.shard_map(
        on_device,
        mesh=mesh,
        in_specs=placed,
        out_specs=(P(("leaf", "grp"), None), P(("leaf", "grp"), None), P("leaf", "grp")),
        check_vma=False,
    )
```

```python
import functools

import jax
import jax.numpy as jnp
from jax import lax
from jax.experimental import pallas as pl
from jax.experimental.pallas import tpu as pltpu
from jax.sharding import PartitionSpec as P

LEVELS = 4
LANES = 128
PANEL = 32
HIGHEST = lax.Precision.HIGHEST


def dot_nn(a, b):
    return lax.dot_general(a, b, (((1,), (0,)), ((), ())), precision=HIGHEST, preferred_element_type=jnp.float32)


def dot_tn(a, b):
    return lax.dot_general(a, b, (((0,), (0,)), ((), ())), precision=HIGHEST, preferred_element_type=jnp.float32)


def dot_nt(a, b):
    return lax.dot_general(a, b, (((1,), (1,)), ((), ())), precision=HIGHEST, preferred_element_type=jnp.float32)


def inverse_of(x):
    guess = pl.reciprocal(x, approx=True)
    guess = guess * (2.0 - x * guess)
    return guess * (2.0 - x * guess)


def inverse_factor(slab):
    groups = PANEL // 8
    tile = (8, LANES)
    lane = lax.broadcasted_iota(jnp.int32, tile, 1)
    row = lax.broadcasted_iota(jnp.int32, tile, 0)
    state = []
    for g in range(groups):
        unit = jnp.where(lane == row + (PANEL + 8 * g), 1.0, 0.0)
        state.append(jnp.where(lane < PANEL, slab[8 * g : 8 * g + 8], unit))
    for q in range(groups):
        cols = {}
        for g in range(q, groups):
            for j in range(8):
                at = 8 * q + j
                cols[g, j] = jnp.broadcast_to(state[g][:, at : at + 1], tile)
        s = {(i, k): jnp.broadcast_to(cols[q, k][i : i + 1], tile) for k in range(8) for i in range(k + 1)}
        pivots = s[0, 0]
        for j in range(0, 8, 2):
            a, b, c = s[j, j], s[j, j + 1], s[j + 1, j + 1]
            det = a * c - b * b
            ra, rdet = inverse_of(a), inverse_of(det)
            ratio, rs = b * ra, a * rdet
            pivots = jnp.where(row >= j, a, pivots)
            pivots = jnp.where(row >= j + 1, det * ra, pivots)
            x, y = {}, {}
            for k in range(j + 2, 8):
                y[k] = (s[j + 1, k] - ratio * s[j, k]) * rs
                x[k] = s[j, k] * ra - ratio * y[k]
            for i in range(j + 2, 8):
                for k in range(i, 8):
                    s[i, k] = s[i, k] - (s[j, i] * x[k] + s[j + 1, i] * y[k])
            upper = jnp.broadcast_to(state[q][j : j + 1], tile)
            lower = jnp.broadcast_to(state[q][j + 1 : j + 2], tile)
            shift = ratio * upper
            line_y = (lower - shift) * rs
            line_x = upper * ra - ratio * line_y
            for g in range(q, groups):
                for k in range(j + 2, 8):
                    cols[g, k] = cols[g, k] - (cols[g, j] * x[k] + cols[g, j + 1] * y[k])
                drop = cols[g, j] * line_x + cols[g, j + 1] * line_y
                if g == q:
                    drop = jnp.where(row > j + 1, drop, jnp.where(row == j + 1, shift, 0.0))
                state[g] = state[g] - drop
        state[q] = state[q] * lax.rsqrt(pivots)
    whole = jnp.concatenate(state, axis=0)
    return whole[:, PANEL : 2 * PANEL]


def merge_kernel(height, slots, ranks, own_b, own_g, own_y, peer_b, peer_g, peer_y, mix_a, mix_b, out_b, out_g, out_y, piv, work, high, full, mix):
    size = own_b.shape[0]
    gen_w = own_g.shape[1]
    first = height == 0
    position = lax.axis_index("leaf")
    upper = (position >> height) % 2 == 1
    base_node = (position >> (height + 1)) << (height + 1)
    low_rank = ranks[base_node + 2**height - 1]
    high_rank = ranks[base_node + 2 ** (height + 1) - 1]
    part = size // len(slots)
    for which, offset, flip in slots:
        index = jnp.bitwise_xor(position, flip) % len(slots)
        mix[pl.ds(pl.multiple_of(index * part, part), part), :] = (mix_b if which else mix_a)[offset : offset + part, :]
    row_ids = lax.broadcasted_iota(jnp.int32, (size, size), 0)
    col_ids = lax.broadcasted_iota(jnp.int32, (size, size), 1)
    mixing = jnp.where((row_ids < high_rank) & (col_ids < low_rank), mix[...], 0.0)
    if first:
        full[...] = peer_b[...]
    else:
        for i in range(size // LANES):
            for j in range(i + 1):
                here, there = slice(i * LANES, (i + 1) * LANES), slice(j * LANES, (j + 1) * LANES)
                full[here, there] = peer_b[here, there]
                if j < i:
                    full[there, here] = peer_b[here, there].T
    high_b = jnp.where(upper, own_b[...], full[...])
    high_g = jnp.where(upper, own_g[...], peer_g[...])
    high_y = jnp.where(upper, own_y[...], peer_y[...])
    low_b = jnp.where(upper, full[...], own_b[...])
    low_g = jnp.where(upper, peer_g[...], own_g[...])
    low_y = jnp.where(upper, peer_y[...], own_y[...])
    if first:
        unit = jnp.where(row_ids == col_ids, 1.0, 0.0)
        high_b = jnp.where((row_ids < high_rank) & (col_ids < high_rank), high_b, unit)
        low_b = jnp.where((row_ids < low_rank) & (col_ids < low_rank), low_b, unit)
        gen_rows = lax.broadcasted_iota(jnp.int32, high_g.shape, 0)
        rhs_rows = lax.broadcasted_iota(jnp.int32, high_y.shape, 0)
        high_g = jnp.where(gen_rows < high_rank, high_g, 0.0)
        low_g = jnp.where(gen_rows < low_rank, low_g, 0.0)
        high_y = jnp.where(rhs_rows < high_rank, high_y, 0.0)
        low_y = jnp.where(rhs_rows < low_rank, low_y, 0.0)
    high[:, :size] = high_b
    high[:, size : size + gen_w] = high_g
    high[:, size + gen_w :] = high_y
    mixed = dot_tn(mixing, high[...])
    high_gen = high[:, size : size + gen_w]
    w_gen = low_g + mixed[:, size : size + gen_w]
    w_rhs = low_y + mixed[:, size + gen_w :]
    coupled = mixed[:, :size] + dot_nt(w_gen, high_gen)
    pivot = low_b + dot_nn(mixed[:, :size], mixing) + dot_nt(w_gen, w_gen)
    diagonal = jnp.where(row_ids == col_ids, pivot, 0.0)
    scale = lax.rsqrt(jnp.sum(diagonal, axis=1, keepdims=True))
    piv[...] = pivot * scale * lax.rsqrt(jnp.sum(diagonal, axis=0, keepdims=True))
    work[:, :size] = coupled * scale
    work[:, size : size + gen_w] = w_gen * scale
    work[:, size + gen_w :] = w_rhs * scale
    high[:, :size] = high[:, :size] + dot_nt(high_gen, high_gen)

    def factor_at(base, q):
        start = pl.multiple_of(base + q * PANEL, PANEL)
        slab = piv[pl.ds(start, PANEL), base : base + LANES]
        return inverse_factor(pltpu.roll(slab, (LANES - q * PANEL) % LANES, 1))

    for chunk in range(size // LANES):
        base, after = chunk * LANES, (chunk + 1) * LANES

        @pl.when(low_rank > base)
        def _(base=base, after=after):
            if base:
                done = piv[base - LANES : base, base:]
                piv[base:, base:] = piv[base:, base:] - dot_tn(done, done)
            inv = factor_at(base, 0)
            if base:
                work[base:, :] = work[base:, :] - dot_tn(done, work[base - LANES : base, :])
            steps = jnp.minimum((low_rank - base + PANEL - 1) // PANEL, LANES // PANEL)

            def wide(q, inv):
                rows = pl.ds(pl.multiple_of(base + q * PANEL, PANEL), PANEL)
                parts = []
                if after < size:
                    part = dot_nn(inv, piv[rows, after:])
                    piv[rows, after:] = part
                    parts.append(part)
                part = dot_nn(inv, work[rows, :])
                work[rows, :] = part
                return parts + [part]

            def panel(q, inv):
                rows = pl.ds(pl.multiple_of(base + q * PANEL, PANEL), PANEL)
                head = dot_nn(inv, piv[rows, base:after])
                ids = lax.broadcasted_iota(jnp.int32, (PANEL, LANES), 1)
                left = jnp.where(ids >= (q + 1) * PANEL, head, 0.0)
                piv[base:after, base:after] = piv[base:after, base:after] - dot_tn(left, head)
                following = factor_at(base, q + 1)
                parts = wide(q, inv)
                if after < size:
                    piv[base:after, after:] = piv[base:after, after:] - dot_tn(left, parts[0])
                work[base:after, :] = work[base:after, :] - dot_tn(left, parts[-1])
                return following

            inv = lax.fori_loop(0, steps - 1, panel, inv)
            wide(steps - 1, inv)

    solved = work[...]
    result = high[...] - dot_tn(solved[:, :size], solved)
    out_b[...] = result[:, :size]
    out_g[...] = result[:, size : size + gen_w]
    out_y[...] = result[:, size + gen_w :]


def merge(height, slots, ranks, own, peer, mix_a, mix_b):
    size, gen_w, rhs_w = own[0].shape[0], own[1].shape[1], own[2].shape[1]
    wide = size + gen_w + rhs_w
    vmem = pl.BlockSpec(memory_space=pltpu.VMEM)
    return pl.pallas_call(
        functools.partial(merge_kernel, height, slots),
        out_shape=[jax.ShapeDtypeStruct(x.shape, jnp.float32) for x in own],
        in_specs=[pl.BlockSpec(memory_space=pltpu.SMEM)] + [vmem] * 8,
        out_specs=[vmem] * 3,
        scratch_shapes=[
            pltpu.VMEM((size, size), jnp.float32),
            pltpu.VMEM((size, wide), jnp.float32),
            pltpu.VMEM((size, wide), jnp.float32),
            pltpu.VMEM((size, size), jnp.float32),
            pltpu.VMEM((size, size), jnp.float32),
        ],
        compiler_params=pltpu.CompilerParams(vmem_limit_bytes=40 * 2**20),
        cost_estimate=pl.CostEstimate(flops=6 * 10**9, bytes_accessed=4 * 2**20, transcendentals=0),
    )(ranks, *own, *peer, mix_a, mix_b)


def flipped(index, step):
    return index + step - 2 * step * ((index // step) % 2)


def greet(devices):
    barrier = pltpu.get_barrier_semaphore()
    for device in devices:
        pl.semaphore_signal(barrier, inc=1, device_id=device, device_id_type=pl.DeviceIdType.MESH)
    pl.semaphore_wait(barrier, len(devices))


class Sender:
    def __init__(self, send, recv):
        self.send, self.recv, self.used = send, recv, 0

    def __call__(self, src, dst, device):
        copy = pltpu.make_async_remote_copy(
            src_ref=src,
            dst_ref=dst,
            send_sem=self.send.at[self.used],
            recv_sem=self.recv.at[self.used],
            device_id=device,
            device_id_type=pl.DeviceIdType.MESH,
        )
        self.used += 1
        copy.start()
        return copy


def first_kernel(diag, gen, rhs, near, later, own_b, own_g, peer_b, peer_g, peer_y, peer_near, peer_later, send, recv, local):
    leaf, core = lax.axis_index("leaf"), lax.axis_index("grp")
    across, over, beside = (flipped(leaf, 1), core), (flipped(leaf, 2), core), (leaf, flipped(core, 1))
    greet([across, over, beside])
    size = own_b.shape[0]
    half = size // 2
    side = core % 2
    mine = pl.ds(pl.multiple_of(side * half, half), half)
    quarter = near.shape[0] // 2
    near_mine = pl.ds(pl.multiple_of(side * quarter, quarter), quarter)
    keep_b = pltpu.make_async_copy(diag, own_b.at[mine], local.at[0])
    keep_g = pltpu.make_async_copy(gen, own_g.at[mine], local.at[1])
    remote = Sender(send, recv)
    far = [
        (remote(diag, peer_b.at[mine], across), peer_b.at[mine]),
        (remote(near.at[near_mine], peer_near.at[near_mine], across), peer_near.at[near_mine]),
        (remote(gen, peer_g.at[mine], across), peer_g.at[mine]),
    ]
    rest = [
        remote(rhs, peer_y, across),
        remote(later, peer_later, over),
        remote(diag, own_b.at[mine], beside),
        remote(gen, own_g.at[mine], beside),
    ]
    keep_b.start()
    keep_g.start()
    for copy, place in far:
        copy.wait_recv()
        rest.append(remote(place, place, beside))
    for copy, place in far:
        copy.wait_send()
    for copy in rest:
        copy.wait()
    keep_b.wait()
    keep_g.wait()


def first_exchange(diag, gen, rhs, near, later):
    size = diag.shape[1]
    vmem = pl.BlockSpec(memory_space=pltpu.VMEM)
    shapes = [(size, size), (size, gen.shape[1]), (size, size), (size, gen.shape[1]), rhs.shape, near.shape, later.shape]
    return pl.pallas_call(
        first_kernel,
        out_shape=[jax.ShapeDtypeStruct(x, jnp.float32) for x in shapes],
        in_specs=[vmem] * 5,
        out_specs=[vmem] * 7,
        scratch_shapes=[pltpu.SemaphoreType.DMA((10,)), pltpu.SemaphoreType.DMA((10,)), pltpu.SemaphoreType.DMA((2,))],
        compiler_params=pltpu.CompilerParams(collective_id=0, vmem_limit_bytes=24 * 2**20, has_side_effects=True),
    )(diag, gen, rhs, near, later)


def pair_kernel(step, b, g, y, peer_b, peer_g, peer_y, send, recv):
    leaf, core = lax.axis_index("leaf"), lax.axis_index("grp")
    across, beside = (flipped(leaf, step), core), (leaf, flipped(core, 1))
    greet([across, beside])
    side = core % 2
    half = g.shape[0] // 2
    mine = pl.ds(pl.multiple_of(side * half, half), half)
    remote = Sender(send, recv)
    far = []
    for t in range(3):
        row = 2 * side + (1 - side) * (0, 1, 1)[t]
        col = t * side + (1 - side) * (0, 0, 1)[t]
        rows = pl.ds(pl.multiple_of(row * LANES, LANES), LANES)
        cols = pl.ds(pl.multiple_of(col * LANES, LANES), LANES)
        far.append((remote(b.at[rows, cols], peer_b.at[rows, cols], across), peer_b.at[rows, cols]))
    far.append((remote(g.at[mine], peer_g.at[mine], across), peer_g.at[mine]))
    rest = [remote(y, peer_y, across)]
    for copy, place in far:
        copy.wait_recv()
        rest.append(remote(place, place, beside))
    for copy, place in far:
        copy.wait_send()
    for copy in rest:
        copy.wait()


def pair_exchange(height, own):
    vmem = pl.BlockSpec(memory_space=pltpu.VMEM)
    return pl.pallas_call(
        functools.partial(pair_kernel, 2**height),
        out_shape=[jax.ShapeDtypeStruct(x.shape, jnp.float32) for x in own],
        in_specs=[vmem] * 3,
        out_specs=[vmem] * 3,
        scratch_shapes=[pltpu.SemaphoreType.DMA((9,)), pltpu.SemaphoreType.DMA((9,))],
        compiler_params=pltpu.CompilerParams(collective_id=height, vmem_limit_bytes=24 * 2**20, has_side_effects=True),
    )(*own)


def swapped(block, axis, bit):
    count = lax.axis_size(axis)
    return lax.ppermute(block, axis, [(low, low ^ 1 << bit) for low in range(count)])


def on_device(diag_block, generator, right_sides, interp_first, interp_second, interp_third, interp_fourth, node_ranks):
    position = lax.axis_index("leaf")
    member = lax.axis_index("grp")
    share = diag_block.shape[0]
    size = diag_block.shape[1]
    near = interp_first
    later = jnp.concatenate([interp_second, interp_third, interp_fourth], axis=0)
    rows = [x.shape[0] for x in (interp_first, interp_second, interp_third, interp_fourth)]
    diag_half, gen_half = diag_block, generator
    if 2 * share != size:
        side = member % 2
        diag_full = lax.all_gather(diag_block, "grp", axis=0, tiled=True)
        gen_full = lax.all_gather(generator, "grp", axis=0, tiled=True)
        diag_half = lax.dynamic_slice_in_dim(diag_full, side * (size // 2), size // 2, 0)
        gen_half = lax.dynamic_slice_in_dim(gen_full, side * (size // 2), size // 2, 0)
    own_b, own_g, peer_b, peer_g, peer_y, peer_near, peer_later = first_exchange(
        diag_half, gen_half, right_sides, near, later
    )
    now = (own_b, own_g, right_sides)
    peer = (peer_b, peer_g, peer_y)
    held, got = near, peer_near
    flips = [0]
    held_next = jnp.concatenate([later, peer_later], axis=0)
    got_next = swapped(held_next, "leaf", 0)
    flips_next = [0, 2]
    for height in range(LEVELS):
        bit = (0, 0, 2, 3)[height]
        width = sum(rows[height:]) if height else rows[0]
        slots = []
        for which in range(2):
            slots += [(which, i * width, flip ^ (which << bit)) for i, flip in enumerate(flips)]
        now = merge(height, slots, node_ranks, now, peer, held, got)
        if height + 1 < LEVELS:
            held, got, flips = held_next, got_next, flips_next
            peer = pair_exchange(height + 1, now)
            if height + 2 < LEVELS:
                skip, wide = rows[height + 1], sum(rows[height + 1 :])
                pieces = []
                for array in (held, got):
                    pieces += [array[i * wide + skip : (i + 1) * wide] for i in range(len(flips))]
                held_next = jnp.concatenate(pieces, axis=0)
                got_next = swapped(held_next, "leaf", height + 2)
                flips_next = flips + [flip ^ (1 << (0, 0, 2, 3)[height + 1]) for flip in flips]
    out_block = lax.dynamic_slice_in_dim(now[0], member % (size // share) * share, share, 0)
    out_gen = lax.dynamic_slice_in_dim(now[1], member % (size // share) * share, share, 0)
    return (out_block, out_gen, now[2])


def solution(mesh):
    placed = (
        P(("leaf", "grp"), None),
        P(("leaf", "grp"), None),
        P("leaf", "grp"),
        P("leaf", None),
        P("leaf", None),
        P("leaf", None),
        P("leaf", None),
        P(),
    )
    return jax.shard_map(
        on_device,
        mesh=mesh,
        in_specs=placed,
        out_specs=(P(("leaf", "grp"), None), P(("leaf", "grp"), None), P("leaf", "grp")),
        check_vma=False,
    )
```

```python
import functools

import jax
import jax.numpy as jnp
from jax import lax
from jax.experimental import pallas as pl
from jax.experimental.pallas import tpu as pltpu
from jax.sharding import PartitionSpec as P

LEVELS = 4
LANES = 128
PANEL = 32
HIGHEST = lax.Precision.HIGHEST


def dot_nn(a, b):
    return lax.dot_general(a, b, (((1,), (0,)), ((), ())), precision=HIGHEST, preferred_element_type=jnp.float32)


def split(x):
    high = x.astype(jnp.bfloat16)
    rest = x - high.astype(jnp.float32)
    middle = rest.astype(jnp.bfloat16)
    return high, middle, (rest - middle.astype(jnp.float32)).astype(jnp.bfloat16)


def dot_six(a, b, axis_a, axis_b):
    ah, am, al = split(a)
    bh, bm, bl = split(b)
    left = jnp.concatenate([ah, ah, am, am, ah, al], axis=axis_a)
    right = jnp.concatenate([bh, bm, bh, bm, bl, bh], axis=axis_b)
    return lax.dot_general(left, right, (((axis_a,), (axis_b,)), ((), ())), preferred_element_type=jnp.float32)


def dot_tn(a, b):
    return dot_six(a, b, 0, 0)


def dot_nt(a, b):
    return dot_six(a, b, 1, 1)


def inverse_of(x):
    guess = pl.reciprocal(x, approx=True)
    guess = guess * (2.0 - x * guess)
    return guess * (2.0 - x * guess)


def inverse_factor(slab):
    groups = PANEL // 8
    tile = (8, LANES)
    lane = lax.broadcasted_iota(jnp.int32, tile, 1)
    row = lax.broadcasted_iota(jnp.int32, tile, 0)
    state = []
    for g in range(groups):
        unit = jnp.where(lane == row + (PANEL + 8 * g), 1.0, 0.0)
        state.append(jnp.where(lane < PANEL, slab[8 * g : 8 * g + 8], unit))
    for q in range(groups):
        cols = {}
        for g in range(q, groups):
            for j in range(8):
                at = 8 * q + j
                cols[g, j] = jnp.broadcast_to(state[g][:, at : at + 1], tile)
        s = {(i, k): jnp.broadcast_to(cols[q, k][i : i + 1], tile) for k in range(8) for i in range(k + 1)}
        pivots = s[0, 0]
        for j in range(0, 8, 2):
            a, b, c = s[j, j], s[j, j + 1], s[j + 1, j + 1]
            det = a * c - b * b
            ra, rdet = inverse_of(a), inverse_of(det)
            ratio, rs = b * ra, a * rdet
            pivots = jnp.where(row >= j, a, pivots)
            pivots = jnp.where(row >= j + 1, det * ra, pivots)
            x, y = {}, {}
            for k in range(j + 2, 8):
                y[k] = (s[j + 1, k] - ratio * s[j, k]) * rs
                x[k] = s[j, k] * ra - ratio * y[k]
            for i in range(j + 2, 8):
                for k in range(i, 8):
                    s[i, k] = s[i, k] - (s[j, i] * x[k] + s[j + 1, i] * y[k])
            upper = jnp.broadcast_to(state[q][j : j + 1], tile)
            lower = jnp.broadcast_to(state[q][j + 1 : j + 2], tile)
            shift = ratio * upper
            line_y = (lower - shift) * rs
            line_x = upper * ra - ratio * line_y
            for g in range(q, groups):
                for k in range(j + 2, 8):
                    cols[g, k] = cols[g, k] - (cols[g, j] * x[k] + cols[g, j + 1] * y[k])
                drop = cols[g, j] * line_x + cols[g, j + 1] * line_y
                if g == q:
                    drop = jnp.where(row > j + 1, drop, jnp.where(row == j + 1, shift, 0.0))
                state[g] = state[g] - drop
        state[q] = state[q] * lax.rsqrt(pivots)
    whole = jnp.concatenate(state, axis=0)
    return whole[:, PANEL : 2 * PANEL]


def merge_kernel(height, slots, ranks, own_b, own_g, own_y, peer_b, peer_g, peer_y, mix_a, mix_b, out_b, out_g, out_y, piv, work, high, full, mix):
    size = own_b.shape[0]
    gen_w = own_g.shape[1]
    first = height == 0
    position = lax.axis_index("leaf")
    upper = (position >> height) % 2 == 1
    base_node = (position >> (height + 1)) << (height + 1)
    low_rank = ranks[base_node + 2**height - 1]
    high_rank = ranks[base_node + 2 ** (height + 1) - 1]
    part = size // len(slots)
    for which, offset, flip in slots:
        index = jnp.bitwise_xor(position, flip) % len(slots)
        mix[pl.ds(pl.multiple_of(index * part, part), part), :] = (mix_b if which else mix_a)[offset : offset + part, :]
    row_ids = lax.broadcasted_iota(jnp.int32, (size, size), 0)
    col_ids = lax.broadcasted_iota(jnp.int32, (size, size), 1)
    mixing = jnp.where((row_ids < high_rank) & (col_ids < low_rank), mix[...], 0.0)
    if first:
        full[...] = peer_b[...]
    else:
        for i in range(size // LANES):
            for j in range(i + 1):
                here, there = slice(i * LANES, (i + 1) * LANES), slice(j * LANES, (j + 1) * LANES)
                full[here, there] = peer_b[here, there]
                if j < i:
                    full[there, here] = peer_b[here, there].T
    high_b = jnp.where(upper, own_b[...], full[...])
    high_g = jnp.where(upper, own_g[...], peer_g[...])
    high_y = jnp.where(upper, own_y[...], peer_y[...])
    low_b = jnp.where(upper, full[...], own_b[...])
    low_g = jnp.where(upper, peer_g[...], own_g[...])
    low_y = jnp.where(upper, peer_y[...], own_y[...])
    if first:
        unit = jnp.where(row_ids == col_ids, 1.0, 0.0)
        high_b = jnp.where((row_ids < high_rank) & (col_ids < high_rank), high_b, unit)
        low_b = jnp.where((row_ids < low_rank) & (col_ids < low_rank), low_b, unit)
        gen_rows = lax.broadcasted_iota(jnp.int32, high_g.shape, 0)
        rhs_rows = lax.broadcasted_iota(jnp.int32, high_y.shape, 0)
        high_g = jnp.where(gen_rows < high_rank, high_g, 0.0)
        low_g = jnp.where(gen_rows < low_rank, low_g, 0.0)
        high_y = jnp.where(rhs_rows < high_rank, high_y, 0.0)
        low_y = jnp.where(rhs_rows < low_rank, low_y, 0.0)
    high[:, :size] = high_b
    high[:, size : size + gen_w] = high_g
    high[:, size + gen_w :] = high_y
    mixed = dot_tn(mixing, high[...])
    high_gen = high[:, size : size + gen_w]
    w_gen = low_g + mixed[:, size : size + gen_w]
    w_rhs = low_y + mixed[:, size + gen_w :]
    coupled = mixed[:, :size] + dot_nt(w_gen, high_gen)
    pivot = low_b + dot_six(mixed[:, :size], mixing, 1, 0) + dot_nt(w_gen, w_gen)
    diagonal = jnp.where(row_ids == col_ids, pivot, 0.0)
    scale = lax.rsqrt(jnp.sum(diagonal, axis=1, keepdims=True))
    piv[...] = pivot * scale * lax.rsqrt(jnp.sum(diagonal, axis=0, keepdims=True))
    work[:, :size] = coupled * scale
    work[:, size : size + gen_w] = w_gen * scale
    work[:, size + gen_w :] = w_rhs * scale
    high[:, :size] = high[:, :size] + dot_nt(high_gen, high_gen)

    def factor_at(base, q):
        start = pl.multiple_of(base + q * PANEL, PANEL)
        slab = piv[pl.ds(start, PANEL), base : base + LANES]
        return inverse_factor(pltpu.roll(slab, (LANES - q * PANEL) % LANES, 1))

    for chunk in range(size // LANES):
        base, after = chunk * LANES, (chunk + 1) * LANES

        @pl.when(low_rank > base)
        def _(base=base, after=after):
            if base:
                done = piv[base - LANES : base, base:]
                piv[base:, base:] = piv[base:, base:] - dot_tn(done, done)
            inv = factor_at(base, 0)
            if base:
                work[base:, :] = work[base:, :] - dot_tn(done, work[base - LANES : base, :])
            steps = jnp.minimum((low_rank - base + PANEL - 1) // PANEL, LANES // PANEL)

            def wide(q, inv):
                rows = pl.ds(pl.multiple_of(base + q * PANEL, PANEL), PANEL)
                parts = []
                if after < size:
                    part = dot_nn(inv, piv[rows, after:])
                    piv[rows, after:] = part
                    parts.append(part)
                part = dot_nn(inv, work[rows, :])
                work[rows, :] = part
                return parts + [part]

            def panel(q, inv):
                rows = pl.ds(pl.multiple_of(base + q * PANEL, PANEL), PANEL)
                head = dot_nn(inv, piv[rows, base:after])
                ids = lax.broadcasted_iota(jnp.int32, (PANEL, LANES), 1)
                left = jnp.where(ids >= (q + 1) * PANEL, head, 0.0)
                piv[base:after, base:after] = piv[base:after, base:after] - dot_tn(left, head)
                following = factor_at(base, q + 1)
                parts = wide(q, inv)
                if after < size:
                    piv[base:after, after:] = piv[base:after, after:] - dot_tn(left, parts[0])
                work[base:after, :] = work[base:after, :] - dot_tn(left, parts[-1])
                return following

            inv = lax.fori_loop(0, steps - 1, panel, inv)
            wide(steps - 1, inv)

    solved = work[...]
    result = high[...] - dot_tn(solved[:, :size], solved)
    out_b[...] = result[:, :size]
    out_g[...] = result[:, size : size + gen_w]
    out_y[...] = result[:, size + gen_w :]


def merge(height, slots, ranks, own, peer, mix_a, mix_b):
    size, gen_w, rhs_w = own[0].shape[0], own[1].shape[1], own[2].shape[1]
    wide = size + gen_w + rhs_w
    vmem = pl.BlockSpec(memory_space=pltpu.VMEM)
    return pl.pallas_call(
        functools.partial(merge_kernel, height, slots),
        out_shape=[jax.ShapeDtypeStruct(x.shape, jnp.float32) for x in own],
        in_specs=[pl.BlockSpec(memory_space=pltpu.SMEM)] + [vmem] * 8,
        out_specs=[vmem] * 3,
        scratch_shapes=[
            pltpu.VMEM((size, size), jnp.float32),
            pltpu.VMEM((size, wide), jnp.float32),
            pltpu.VMEM((size, wide), jnp.float32),
            pltpu.VMEM((size, size), jnp.float32),
            pltpu.VMEM((size, size), jnp.float32),
        ],
        compiler_params=pltpu.CompilerParams(vmem_limit_bytes=40 * 2**20),
        cost_estimate=pl.CostEstimate(flops=6 * 10**9, bytes_accessed=4 * 2**20, transcendentals=0),
    )(ranks, *own, *peer, mix_a, mix_b)


def flipped(index, step):
    return index + step - 2 * step * ((index // step) % 2)


def greet(devices):
    barrier = pltpu.get_barrier_semaphore()
    for device in devices:
        pl.semaphore_signal(barrier, inc=1, device_id=device, device_id_type=pl.DeviceIdType.MESH)
    pl.semaphore_wait(barrier, len(devices))


class Sender:
    def __init__(self, send, recv):
        self.send, self.recv, self.used = send, recv, 0

    def __call__(self, src, dst, device):
        copy = pltpu.make_async_remote_copy(
            src_ref=src,
            dst_ref=dst,
            send_sem=self.send.at[self.used],
            recv_sem=self.recv.at[self.used],
            device_id=device,
            device_id_type=pl.DeviceIdType.MESH,
        )
        self.used += 1
        copy.start()
        return copy


def first_kernel(diag, gen, rhs, near, later, own_b, own_g, peer_b, peer_g, peer_y, peer_near, peer_later, send, recv, local):
    leaf, core = lax.axis_index("leaf"), lax.axis_index("grp")
    across, over, beside = (flipped(leaf, 1), core), (flipped(leaf, 2), core), (leaf, flipped(core, 1))
    greet([across, over, beside])
    size = own_b.shape[0]
    half = size // 2
    side = core % 2
    mine = pl.ds(pl.multiple_of(side * half, half), half)
    quarter = near.shape[0] // 2
    near_mine = pl.ds(pl.multiple_of(side * quarter, quarter), quarter)
    keep_b = pltpu.make_async_copy(diag, own_b.at[mine], local.at[0])
    keep_g = pltpu.make_async_copy(gen, own_g.at[mine], local.at[1])
    remote = Sender(send, recv)
    far = [
        (remote(diag, peer_b.at[mine], across), peer_b.at[mine]),
        (remote(near.at[near_mine], peer_near.at[near_mine], across), peer_near.at[near_mine]),
        (remote(gen, peer_g.at[mine], across), peer_g.at[mine]),
    ]
    rest = [
        remote(rhs, peer_y, across),
        remote(later, peer_later, over),
        remote(diag, own_b.at[mine], beside),
        remote(gen, own_g.at[mine], beside),
    ]
    keep_b.start()
    keep_g.start()
    for copy, place in far:
        copy.wait_recv()
        rest.append(remote(place, place, beside))
    for copy, place in far:
        copy.wait_send()
    for copy in rest:
        copy.wait()
    keep_b.wait()
    keep_g.wait()


def first_exchange(diag, gen, rhs, near, later):
    size = diag.shape[1]
    vmem = pl.BlockSpec(memory_space=pltpu.VMEM)
    shapes = [(size, size), (size, gen.shape[1]), (size, size), (size, gen.shape[1]), rhs.shape, near.shape, later.shape]
    return pl.pallas_call(
        first_kernel,
        out_shape=[jax.ShapeDtypeStruct(x, jnp.float32) for x in shapes],
        in_specs=[vmem] * 5,
        out_specs=[vmem] * 7,
        scratch_shapes=[pltpu.SemaphoreType.DMA((10,)), pltpu.SemaphoreType.DMA((10,)), pltpu.SemaphoreType.DMA((2,))],
        compiler_params=pltpu.CompilerParams(collective_id=0, vmem_limit_bytes=24 * 2**20, has_side_effects=True),
    )(diag, gen, rhs, near, later)


def pair_kernel(step, b, g, y, peer_b, peer_g, peer_y, send, recv):
    leaf, core = lax.axis_index("leaf"), lax.axis_index("grp")
    across, beside = (flipped(leaf, step), core), (leaf, flipped(core, 1))
    greet([across, beside])
    side = core % 2
    half = g.shape[0] // 2
    mine = pl.ds(pl.multiple_of(side * half, half), half)
    remote = Sender(send, recv)
    far = []
    for t in range(3):
        row = 2 * side + (1 - side) * (0, 1, 1)[t]
        col = t * side + (1 - side) * (0, 0, 1)[t]
        rows = pl.ds(pl.multiple_of(row * LANES, LANES), LANES)
        cols = pl.ds(pl.multiple_of(col * LANES, LANES), LANES)
        far.append((remote(b.at[rows, cols], peer_b.at[rows, cols], across), peer_b.at[rows, cols]))
    far.append((remote(g.at[mine], peer_g.at[mine], across), peer_g.at[mine]))
    rest = [remote(y, peer_y, across)]
    for copy, place in far:
        copy.wait_recv()
        rest.append(remote(place, place, beside))
    for copy, place in far:
        copy.wait_send()
    for copy in rest:
        copy.wait()


def pair_exchange(height, own):
    vmem = pl.BlockSpec(memory_space=pltpu.VMEM)
    return pl.pallas_call(
        functools.partial(pair_kernel, 2**height),
        out_shape=[jax.ShapeDtypeStruct(x.shape, jnp.float32) for x in own],
        in_specs=[vmem] * 3,
        out_specs=[vmem] * 3,
        scratch_shapes=[pltpu.SemaphoreType.DMA((9,)), pltpu.SemaphoreType.DMA((9,))],
        compiler_params=pltpu.CompilerParams(collective_id=height, vmem_limit_bytes=24 * 2**20, has_side_effects=True),
    )(*own)


def swapped(block, axis, bit):
    count = lax.axis_size(axis)
    return lax.ppermute(block, axis, [(low, low ^ 1 << bit) for low in range(count)])


def on_device(diag_block, generator, right_sides, interp_first, interp_second, interp_third, interp_fourth, node_ranks):
    position = lax.axis_index("leaf")
    member = lax.axis_index("grp")
    share = diag_block.shape[0]
    size = diag_block.shape[1]
    near = interp_first
    later = jnp.concatenate([interp_second, interp_third, interp_fourth], axis=0)
    rows = [x.shape[0] for x in (interp_first, interp_second, interp_third, interp_fourth)]
    diag_half, gen_half = diag_block, generator
    if 2 * share != size:
        side = member % 2
        diag_full = lax.all_gather(diag_block, "grp", axis=0, tiled=True)
        gen_full = lax.all_gather(generator, "grp", axis=0, tiled=True)
        diag_half = lax.dynamic_slice_in_dim(diag_full, side * (size // 2), size // 2, 0)
        gen_half = lax.dynamic_slice_in_dim(gen_full, side * (size // 2), size // 2, 0)
    own_b, own_g, peer_b, peer_g, peer_y, peer_near, peer_later = first_exchange(
        diag_half, gen_half, right_sides, near, later
    )
    now = (own_b, own_g, right_sides)
    peer = (peer_b, peer_g, peer_y)
    held, got = near, peer_near
    flips = [0]
    held_next = jnp.concatenate([later, peer_later], axis=0)
    got_next = swapped(held_next, "leaf", 0)
    flips_next = [0, 2]
    for height in range(LEVELS):
        bit = (0, 0, 2, 3)[height]
        width = sum(rows[height:]) if height else rows[0]
        slots = []
        for which in range(2):
            slots += [(which, i * width, flip ^ (which << bit)) for i, flip in enumerate(flips)]
        now = merge(height, slots, node_ranks, now, peer, held, got)
        if height + 1 < LEVELS:
            held, got, flips = held_next, got_next, flips_next
            peer = pair_exchange(height + 1, now)
            if height + 2 < LEVELS:
                skip, wide = rows[height + 1], sum(rows[height + 1 :])
                pieces = []
                for array in (held, got):
                    pieces += [array[i * wide + skip : (i + 1) * wide] for i in range(len(flips))]
                held_next = jnp.concatenate(pieces, axis=0)
                got_next = swapped(held_next, "leaf", height + 2)
                flips_next = flips + [flip ^ (1 << (0, 0, 2, 3)[height + 1]) for flip in flips]
    out_block = lax.dynamic_slice_in_dim(now[0], member % (size // share) * share, share, 0)
    out_gen = lax.dynamic_slice_in_dim(now[1], member % (size // share) * share, share, 0)
    return (out_block, out_gen, now[2])


def solution(mesh):
    placed = (
        P(("leaf", "grp"), None),
        P(("leaf", "grp"), None),
        P("leaf", "grp"),
        P("leaf", None),
        P("leaf", None),
        P("leaf", None),
        P("leaf", None),
        P(),
    )
    return jax.shard_map(
        on_device,
        mesh=mesh,
        in_specs=placed,
        out_specs=(P(("leaf", "grp"), None), P(("leaf", "grp"), None), P("leaf", "grp")),
        check_vma=False,
    )
```
